512 devices in a mesh: blk: 32 (over x_lo, z), grp: 16 (over x_hi, y, core).
Axes of the slice: x: 4 (x_hi: 2, x_lo: 2; x = x_hi * 2 + x_lo), y: 4, z: 16, core: 2. Of those that a mesh axis runs over, the one named last changes fastest.
Arguments:
- image_emb: bfloat16 [57344, 1152], P(('blk', 'grp')), may hold values from -0.625 to 0.625
- text_held: bfloat16 [57344, 1152], P(('blk', 'grp')), may hold values from -0.625 to 0.625
- text_grad_acc: float32 [57344, 1152], P(('blk', 'grp')), may hold values from -6 to 6
- text_loss_acc: float32 [57344], P(('blk', 'grp')), may hold values from 0 to 2
- match: int32 [57344], P('blk'), may hold values from 0 to 57343, each once
- step: int32 [1], replicated, may hold values from 0 to 999999
- scale: float32 [1], replicated, may hold values from 6 to 14
- bias: float32 [1], replicated, may hold values from -6 to -3
Outputs:
- image_grad: float32 [57344, 1152], P(('blk', 'grp'))
- text_grad_out: float32 [57344, 1152], P(('blk', 'grp'))
- text_loss_out: float32 [57344], P(('blk', 'grp'))
The draws below stay inside these ranges and needn't reach their ends.
Inputs may be any that keep to these rules, and one draw needn't show every extreme that they name: match holds every text index exactly once.
All inputs are finite; a program needn't handle non-finite values.
Results may differ from the reference program's by a relative error of at most 0.014.
Values may be sent and summed in bfloat16 or wider, within the bound.
No kernel may reach another device: no remote copies, remote signals or barrier semaphores. Data moves between devices by JAX's collectives and lax.ppermute only.
A program may use at most 64 MiB of HBM per device.

```python
import jax
import jax.numpy as jnp
from jax import lax

D = 1152
ROWS = 112
IMAGES = 57344
TEXTS = 57344
N_BLK = 32
N_GRP = 16


def block_levels(rng, extent, shards, smallest, top_value):
    gain = 1.0
    for dim, shards_of in shards:
        draws = jax.random.uniform(jax.random.fold_in(jax.random.fold_in(rng, 6), dim), (shards_of,), jnp.float32, smallest / len(shards), top_value / len(shards))
        gain = gain * jnp.repeat(jnp.exp(draws), extent[dim] // shards_of).reshape((-1,) + (1,) * (len(extent) - 1 - dim))
    return gain


def bell_draw(stream_key, extent, deviation, limit, cuts=(), kind=jnp.bfloat16):
    array = deviation * jax.random.normal(stream_key, extent, jnp.float32)
    if cuts:
        array = array * block_levels(stream_key, extent, cuts, -0.22, 0.18)
    return jnp.clip(array, -limit, limit).astype(kind)


def setup_inputs(seed: int = 0) -> dict:
    keys = jax.random.split(jax.random.key(seed), 9)
    image_emb = bell_draw(keys[0], (IMAGES, D), 0.045, 0.625, ((0, 512),))
    text_held = bell_draw(keys[1], (TEXTS, D), 0.045, 0.625, ((0, 512),))
    text_grad_acc = bell_draw(keys[2], (TEXTS, D), 0.5, 6.0, ((0, 512),), jnp.float32)
    text_loss_acc = jnp.clip(2.0 * jax.random.uniform(keys[3], (TEXTS,), jnp.float32) ** block_levels(keys[3], (TEXTS,), ((0, 512),), -0.2, 0.2), 0.0, 2.0)
    match = jax.random.permutation(keys[4], TEXTS).astype(jnp.int32)
    step = jax.random.randint(keys[5], (1,), 0, 1000000).astype(jnp.int32)
    scale = jnp.clip(jax.random.uniform(keys[6], (1,), jnp.float32, 6.0, 14.0), 6.0, 14.0)
    bias = jnp.clip(jax.random.uniform(keys[7], (1,), jnp.float32, -6.0, -3.0), -6.0, -3.0)
    return dict(image_emb=image_emb, text_held=text_held, text_grad_acc=text_grad_acc, text_loss_acc=text_loss_acc, match=match, step=step, scale=scale, bias=bias)


def reference(image_emb, text_held, text_grad_acc, text_loss_acc, match, step, scale, bias):
    nblk = N_BLK
    span = N_GRP * ROWS
    factor = scale[0]
    offset = bias[0]
    images = image_emb.reshape(nblk, span, D)
    held = text_held.reshape(nblk, N_GRP, ROWS, D)
    labels_all = match.reshape(nblk, span)
    within = jnp.arange(span, dtype=jnp.int32).reshape(N_GRP, ROWS)

    def group(index):
        images_here = images[index].astype(jnp.float32)
        labels = labels_all[index]
        image_sum = jnp.zeros((N_GRP, span, D), jnp.float32)
        results = []
        for lag in (0, 1):
            source = jnp.mod(index - lag, nblk).astype(jnp.int32)
            texts = held[source].astype(jnp.float32)
            anchor = jnp.mod(index - lag - step[0], nblk).astype(jnp.int32)
            columns = anchor * span + within
            product = jnp.einsum("grd,id->gri", texts, images_here)
            logits = factor * product + offset
            paired = columns[:, :, None] == labels[None, None, :]
            signs = jnp.where(paired, 1.0, -1.0)
            lost = jnp.sum(jax.nn.softplus(-signs * logits), axis=2) / span
            weights = (jax.nn.sigmoid(logits) - paired.astype(jnp.float32)).astype(jnp.bfloat16)
            weights = lax.optimization_barrier(weights).astype(jnp.float32)
            text_term = factor * jnp.einsum("gri,id->grd", weights, images_here)
            image_sum = image_sum + factor * jnp.einsum("gri,grd->gid", weights, texts)
            results.append((text_term, lost))
        rounded = lax.optimization_barrier(image_sum.astype(jnp.bfloat16)).astype(jnp.float32)
        image_part = jnp.sum(rounded, axis=0)
        return image_part, results[0][0], results[0][1], results[1][0], results[1][1]

    image_part, grad_first, loss_first, grad_second, loss_second = lax.map(group, jnp.arange(nblk, dtype=jnp.int32))
    image_grad = image_part.reshape(IMAGES, D)
    middle = text_grad_acc.reshape(nblk, N_GRP, ROWS, D) + grad_first
    middle_loss = text_loss_acc.reshape(nblk, N_GRP, ROWS) + loss_first
    text_grad_out = (jnp.roll(middle, 1, axis=0) + grad_second).reshape(TEXTS, D)
    text_loss_out = (jnp.roll(middle_loss, 1, axis=0) + loss_second).reshape(TEXTS)
    return image_grad, text_grad_out, text_loss_out
```

```python
import jax
import jax.numpy as jnp
from jax import lax
from jax.sharding import PartitionSpec as P


NBLK = 32
XH, Y, CORE = 2, 4, 2


def spot(xh, y, core):
    return (xh * Y + y) * CORE + core


def member_route(move):
    return [
        (spot(xh, y, c), spot(*move(xh, y, c)))
        for xh in range(XH)
        for y in range(Y)
        for c in range(CORE)
    ]


def across_x(xh, y, c):
    return (1 - xh, y, c)


def across_core(xh, y, c):
    return (xh, y, 1 - c)


def along_y(steps):
    return lambda xh, y, c: (xh, (y + steps) % Y, c)


def stay(xh, y, c):
    return (xh, y, c)


def to_member(block, move):
    return lax.ppermute(block, "grp", member_route(move))


def to_next_group(block, move):
    ngrp = XH * Y * CORE
    route = [
        (b * ngrp + s, ((b + 1) % NBLK) * ngrp + t)
        for b in range(NBLK)
        for s, t in member_route(move)
    ]
    return lax.ppermute(block, ("blk", "grp"), route)


def gather_y(block):
    groups = [[spot(xh, y, c) for y in range(Y)] for xh in range(XH) for c in range(CORE)]
    return lax.all_gather(block, "grp", axis_index_groups=groups, tiled=True)


def tile(texts, columns, images, labels, factor, offset):
    product = lax.dot_general(
        texts, images, (((1,), (1,)), ((), ())), preferred_element_type=jnp.float32
    )
    logits = factor * product + offset
    paired = columns[:, None] == labels[None, :]
    turned = jnp.where(paired, -logits, logits)
    lost = jnp.sum(jax.nn.softplus(turned), axis=1)
    sig = jax.nn.sigmoid(turned)
    weights = jnp.where(paired, -sig, sig).astype(jnp.bfloat16)
    return weights, lost


def on_device(image_emb, text_held, text_grad_acc, text_loss_acc, match, step, scale, bias):
    rows, width = text_held.shape
    ngrp = XH * Y * CORE
    span = ngrp * rows
    here = lax.axis_index("blk")
    member = lax.axis_index("grp")
    xh = member // (Y * CORE)
    y = (member // CORE) % Y
    core = member % CORE
    factor = scale[0]
    offset = bias[0]

    text_z = to_next_group(text_held, stay)
    text_d = to_next_group(text_held, across_x)
    text_x = to_member(text_held, across_x)
    images_own = gather_y(image_emb)
    images_other = to_member(images_own, across_core)

    texts = jnp.concatenate([text_held, text_x, text_z, text_d], axis=0)
    ids = jnp.arange(rows, dtype=jnp.int32)
    partner = member ^ (Y * CORE)
    first = jnp.mod(here - step[0], NBLK) * span
    second = jnp.mod(here - step[0] - 1, NBLK) * span
    columns = jnp.concatenate(
        [
            first + member * rows + ids,
            first + partner * rows + ids,
            second + member * rows + ids,
            second + partner * rows + ids,
        ]
    )
    labels = match.reshape(XH, Y, CORE, rows)
    labels = lax.dynamic_index_in_dim(labels, xh, 0, keepdims=False)
    labels_own = lax.dynamic_index_in_dim(labels, core, 1, keepdims=False).reshape(-1)
    labels_other = lax.dynamic_index_in_dim(labels, 1 - core, 1, keepdims=False).reshape(-1)

    w_own, lost_own = tile(texts, columns, images_own, labels_own, factor, offset)
    w_other, lost_other = tile(texts, columns, images_other, labels_other, factor, offset)
    lost = (lost_own + lost_other) / span

    def image_part(w):
        return factor * lax.dot_general(
            w, texts, (((0,), (0,)), ((), ())), preferred_element_type=jnp.float32
        )

    sent = to_member(image_part(w_other).astype(jnp.bfloat16), across_core)
    text_term = factor * (
        jnp.dot(w_own, images_own, preferred_element_type=jnp.float32)
        + jnp.dot(w_other, images_other, preferred_element_type=jnp.float32)
    )

    def packed(grad, loss):
        tail = jnp.zeros((16, width), jnp.bfloat16)
        tail = tail.at[0, :rows].set(loss.astype(jnp.bfloat16))
        return jnp.concatenate([grad.astype(jnp.bfloat16), tail], axis=0)

    def part(i):
        return text_term[i * rows : (i + 1) * rows], lost[i * rows : (i + 1) * rows]

    grad0, loss0 = part(0)
    from_z = to_next_group(packed(text_grad_acc + grad0, text_loss_acc + loss0), stay)
    from_d = to_next_group(packed(*part(1)), across_x)
    from_x = to_member(packed(*part(3)), across_x)

    image_sum = image_part(w_own) + sent.astype(jnp.float32)
    image_sum = image_sum.reshape(Y, rows, width)

    def block_for(steps):
        return lax.dynamic_index_in_dim(image_sum, (y + steps) % Y, 0, keepdims=False)

    image_grad = block_for(0)
    for steps in (1, 2, 3):
        moved = to_member(block_for(steps).astype(jnp.bfloat16), along_y(steps))
        image_grad = image_grad + moved.astype(jnp.float32)

    grad2, loss2 = part(2)
    text_grad_out = grad2
    text_loss_out = loss2
    for arrived in (from_z, from_d, from_x):
        text_grad_out = text_grad_out + arrived[:rows].astype(jnp.float32)
        text_loss_out = text_loss_out + arrived[rows, :rows].astype(jnp.float32)
    return (image_grad, text_grad_out, text_loss_out)


def solution(mesh):
    placed = (
        P(("blk", "grp"), None),
        P(("blk", "grp"), None),
        P(("blk", "grp"), None),
        P(("blk", "grp")),
        P("blk"),
        P(),
        P(),
        P(),
    )
    return jax.shard_map(
        on_device,
        mesh=mesh,
        in_specs=placed,
        out_specs=(P(("blk", "grp"), None), P(("blk", "grp"), None), P(("blk", "grp"))),
        check_vma=False,
    )
```

```python
import functools

import jax
import jax.numpy as jnp
from jax import lax
from jax.experimental import pallas as pl
from jax.experimental.pallas import tpu as pltpu
from jax.sharding import PartitionSpec as P


NBLK = 32
XH, Y, CORE = 2, 4, 2
ROWS = 112
SETS = Y * ROWS
SPAN = XH * Y * CORE * ROWS
TAIL = 16
LOG2E = 1.4426950408889634
LN2 = 0.6931471805599453
CHUNK = 32
Y_ORDER = (1, 2, 3)
F32 = jnp.float32
BF16 = jnp.bfloat16


def spot(xh, y, core):
    return (xh * Y + y) * CORE + core


def member_route(move):
    return [
        (spot(xh, y, c), spot(*move(xh, y, c)))
        for xh in range(XH)
        for y in range(Y)
        for c in range(CORE)
    ]


def across_x(xh, y, c):
    return (1 - xh, y, c)


def across_core(xh, y, c):
    return (xh, y, 1 - c)


def along_y(steps):
    return lambda xh, y, c: (xh, (y + steps) % Y, c)


def stay(xh, y, c):
    return (xh, y, c)


def to_member(block, move):
    return lax.ppermute(block, "grp", member_route(move))


def to_next_group(block, move):
    ngrp = XH * Y * CORE
    route = [
        (b * ngrp + s, ((b + 1) % NBLK) * ngrp + t)
        for b in range(NBLK)
        for s, t in member_route(move)
    ]
    return lax.ppermute(block, ("blk", "grp"), route)


def gather_y(block):
    groups = [[spot(xh, y, c) for y in range(Y)] for xh in range(XH) for c in range(CORE)]
    return lax.all_gather(block, "grp", axis_index_groups=groups, tiled=True)


VMEM = pl.BlockSpec(memory_space=pltpu.VMEM)
HBM = pl.BlockSpec(memory_space=pltpu.HBM)


def call(body, outs, ins, flops, scratch=(), far=0):
    size = sum(x.size * x.dtype.itemsize for x in [*ins, *outs])
    return pl.pallas_call(
        body,
        out_shape=outs,
        in_specs=[HBM] * far + [VMEM] * (len(ins) - far),
        out_specs=[VMEM] * len(outs),
        scratch_shapes=list(scratch),
        cost_estimate=pl.CostEstimate(flops=flops, bytes_accessed=size, transcendentals=0),
        compiler_params=pltpu.CompilerParams(vmem_limit_bytes=12 * 1024 * 1024),
    )(*ins)


def shape(rows, cols, dtype):
    return jax.ShapeDtypeStruct((rows, cols), dtype)


def labels_of(match_ref, member, other):
    core = (member ^ other) & (CORE - 1)
    xh = member // (Y * CORE)
    lane = lax.broadcasted_iota(jnp.int32, (8, 128), 1)
    last = match_ref.shape[0] - 1
    tiles = []
    for q in range(-(-SETS // 128)):
        tile = jnp.zeros((8, 128), jnp.int32)
        for y in range(q * 128 // ROWS, min(Y - 1, (q * 128 + 127) // ROWS) + 1):
            shift = ROWS * (xh * Y * CORE + core + y)
            row = q + shift // 128
            turn = shift % 128
            pieces = []
            for r in (row, row + 1):
                piece = match_ref[pl.ds(jnp.minimum(r, last), 1), :]
                piece = jnp.broadcast_to(piece, (8, 128))
                pieces.append(pltpu.roll(piece, (128 - turn) % 128, 1))
            found = jnp.where(lane < 128 - turn, pieces[0], pieces[1])
            here = q * 128 + lane
            tile = jnp.where((here >= y * ROWS) & (here < (y + 1) * ROWS), found, tile)
        tiles.append(tile)
    return jnp.concatenate(tiles, axis=1)[0:1, :SETS]


def weigh(s_ref, labels, place, step, scale, bias, w_ref, lost_ref, first):
    here, member = place
    factor, offset = scale * LOG2E, bias * LOG2E
    turned = (here - step) & (NBLK - 1)
    behind = (turned - 1) & (NBLK - 1)
    partner = member ^ (Y * CORE)
    bases = [
        turned * SPAN + member * ROWS,
        turned * SPAN + partner * ROWS - ROWS,
        behind * SPAN + member * ROWS - 2 * ROWS,
        behind * SPAN + partner * ROWS - 3 * ROWS,
    ]

    def chunk(i, carry):
        start = pl.multiple_of(i * CHUNK, CHUNK)
        rows = start + lax.broadcasted_iota(jnp.int32, (CHUNK, 1), 0)
        base = jnp.where(
            rows < 2 * ROWS,
            jnp.where(rows < ROWS, bases[0], bases[1]),
            jnp.where(rows < 3 * ROWS, bases[2], bases[3]),
        )
        logits = factor * s_ref[pl.ds(start, CHUNK), :] + offset
        paired = (rows + base) == labels
        t = jnp.where(paired, -logits, logits)
        e = jnp.exp2(-jnp.abs(t))
        more = jnp.where(e < 1e-4, LOG2E * e, jnp.log2(1.0 + e))
        lost = jnp.maximum(t, 0.0) + more
        sig = jnp.exp2(t - lost)
        w_ref[pl.ds(start, CHUNK), :] = jnp.where(paired, -sig, sig).astype(BF16)
        total = jnp.sum(lost, axis=1, keepdims=True)
        if not first:
            total = total + lost_ref[pl.ds(start, CHUNK), :]
        lost_ref[pl.ds(start, CHUNK), :] = total
        return carry

    lax.fori_loop(0, 2 * XH * ROWS // CHUNK, chunk, 0, unroll=True)


def logits_of(texts, images):
    return lax.dot_general(texts, images, (((1,), (1,)), ((), ())), preferred_element_type=F32)


def image_part(weights, texts):
    return lax.dot_general(weights, texts, (((0,), (0,)), ((), ())), preferred_element_type=F32)


def here_and_member():
    return lax.axis_index("blk"), lax.axis_index("grp")


def fetch(pairs, sems):
    copies = [pltpu.make_async_copy(a, b, sems.at[i]) for i, (a, b) in enumerate(pairs)]
    for copy in copies:
        copy.start()
    return copies


def first_half(
    step, scale, bias, match, t0, t1, t2, t3, images, texts, w, part, lost,
    s, match_v, step_s, scale_s, bias_s, sems,
):
    copies = fetch(
        [(t0, texts.at[:ROWS, :]), (match, match_v), (step, step_s), (scale, scale_s), (bias, bias_s)],
        sems,
    )
    for i, t in enumerate((t1, t2, t3)):
        texts[(i + 1) * ROWS : (i + 2) * ROWS, :] = t[...]
    copies[0].wait()
    s[...] = logits_of(texts[...], images[...])
    for copy in copies[1:]:
        copy.wait()
    place = here_and_member()
    labels = labels_of(match_v, place[1], 0)
    weigh(s, labels, place, step_s[0], scale_s[0], bias_s[0], w, lost, True)
    part[...] = jnp.dot(w[...], images[...], preferred_element_type=F32)


def row_of(column):
    r = lax.broadcasted_iota(jnp.int32, (ROWS, 128), 0)
    c = lax.broadcasted_iota(jnp.int32, (ROWS, 128), 1)
    return jnp.sum(jnp.where(r == c, column, 0.0), axis=0, keepdims=True)


def second_half(
    step, scale, bias, match, texts, images, part, lost, acc, loss_acc,
    w, sent, late_rows, s, lost_all, match_v, step_s, scale_s, bias_s, sems,
):
    copies = fetch([(match, match_v), (step, step_s), (scale, scale_s), (bias, bias_s)], sems)
    s[...] = logits_of(texts[...], images[...])
    lost_all[...] = lost[...]
    for copy in copies:
        copy.wait()
    place = here_and_member()
    factor = scale_s[0]
    labels = labels_of(match_v, place[1], 1)
    weigh(s, labels, place, step_s[0], factor, bias_s[0], w, lost_all, False)
    grad = jnp.dot(w[: 2 * ROWS, :], images[...], preferred_element_type=F32)
    grad = factor * (grad + part[: 2 * ROWS, :])
    sent[:ROWS, :] = (acc[...] + grad[:ROWS]).astype(BF16)
    sent[ROWS : 2 * ROWS, :] = grad[ROWS:].astype(BF16)
    rows = [row_of(lost_all[i * ROWS : (i + 1) * ROWS, :]) * (LN2 / SPAN) for i in range(4)]
    at = lax.broadcasted_iota(jnp.int32, (TAIL, 128), 0)
    tail = jnp.where(at == 0, rows[0], jnp.where(at == 1, rows[1], 0.0))
    at = lax.broadcasted_iota(jnp.int32, (TAIL, ROWS), 0)
    tail = tail[:, :ROWS] + jnp.where(at == 0, loss_acc[...], 0.0)
    sent[2 * ROWS :, :] = jnp.zeros((TAIL, sent.shape[1]), BF16)
    sent[2 * ROWS :, :ROWS] = tail.astype(BF16)
    at = lax.broadcasted_iota(jnp.int32, (8, 128), 0)
    late_rows[...] = jnp.where(at == 0, rows[2], jnp.where(at == 1, rows[3], factor))


def image_other(late_rows, w, texts, out):
    out[...] = (late_rows[2:3, 0:1] * image_part(w[...], texts[...])).astype(BF16)


def rest(late_rows, w_own, w_other, texts, images, part, image_own, late):
    factor = late_rows[2:3, 0:1]
    image_own[...] = factor * image_part(w_own[...], texts[...])
    grad = jnp.dot(w_other[2 * ROWS :, :], images[...], preferred_element_type=F32)
    late[...] = factor * (grad + part[2 * ROWS :, :])


def image_sum(steps, own, came, *refs):
    y = (lax.axis_index("grp") // CORE) & (Y - 1)
    for step, out in zip(steps, refs[-len(steps) :]):
        start = pl.multiple_of(((y + step) & (Y - 1)) * ROWS, 16)
        rows = pl.ds(start, ROWS)
        out[...] = (own[rows, :] + came[rows, :].astype(F32)).astype(out.dtype)


def across(late, late_rows, came, token, sent):
    sent[:ROWS, :] = (late[ROWS:, :] + came[ROWS : 2 * ROWS, :].astype(F32)).astype(BF16)
    sent[ROWS:, :] = jnp.zeros((TAIL, sent.shape[1]), BF16)
    tail = came[2 * ROWS :, :128].astype(F32)
    sent[ROWS:, :128] = (tail[1:2, :] + late_rows[1:2, :] + jnp.zeros((TAIL, 128), F32)).astype(BF16)


def image_end(kept, one, two, three, out):
    out[...] = kept[...] + one[...].astype(F32) + two[...].astype(F32) + three[...].astype(F32)


def text_end(late, late_rows, came, crossed, grad, loss):
    grad[...] = late[:ROWS, :] + came[:ROWS, :].astype(F32) + crossed[:ROWS, :].astype(F32)
    ahead = came[2 * ROWS :, :128].astype(F32)
    beside = crossed[ROWS:, :128].astype(F32)
    loss[...] = (late_rows[0:1, :] + ahead[0:1, :] + beside[0:1, :])[:, :ROWS]


def on_device(image_emb, text_held, text_grad_acc, text_loss_acc, match, step, scale, bias):
    width = text_held.shape[1]

    text_z = to_next_group(text_held, stay)
    text_d = to_next_group(text_held, across_x)
    text_x = to_member(text_held, across_x)
    images = gather_y(image_emb)
    images_other = to_member(images, across_core)

    match = match.reshape(-1, 128)
    count = 2 * XH * ROWS
    big = 2 * count * SETS * width
    scratch = [
        pltpu.VMEM(match.shape, jnp.int32),
        pltpu.SMEM((1,), jnp.int32),
        pltpu.SMEM((1,), F32),
        pltpu.SMEM((1,), F32),
        pltpu.SemaphoreType.DMA((5,)),
    ]
    texts, w_own, part, lost = call(
        first_half,
        [shape(count, width, BF16), shape(count, SETS, BF16), shape(count, width, F32), shape(count, 1, F32)],
        [step, scale, bias, match, text_held, text_x, text_z, text_d, images],
        40 * big,
        [pltpu.VMEM((count, SETS), F32), *scratch],
        far=5,
    )
    w_other, ahead, late_rows = call(
        second_half,
        [shape(count, SETS, BF16), shape(2 * ROWS + TAIL, width, BF16), shape(8, 128, F32)],
        [step, scale, bias, match, texts, images_other, part, lost, text_grad_acc, text_loss_acc.reshape(1, ROWS)],
        2 * big,
        [pltpu.VMEM((count, SETS), F32), pltpu.VMEM((count, 1), F32), *scratch],
        far=4,
    )
    came = to_next_group(ahead, stay)
    (other,) = call(image_other, [shape(SETS, width, BF16)], [late_rows, w_other, texts], 20 * big)
    other_came = to_member(other, across_core)
    image_own, late = call(
        rest,
        [shape(SETS, width, F32), shape(2 * ROWS, width, F32)],
        [late_rows, w_own, w_other, texts, images_other, part],
        20 * big,
    )
    block = shape(ROWS, width, BF16)
    arrived = []
    token = ()
    for step_y in Y_ORDER:
        steps = (step_y,) if step_y != Y_ORDER[-1] else (step_y, 0)
        outs = [block, shape(ROWS, width, F32)][: len(steps)]
        sums = call(functools.partial(image_sum, steps), outs, [image_own, other_came, *token], 20 * big)
        arrived.append(to_member(sums[0], along_y(step_y)))
        token = sums[-1:]
    kept = token[0]
    (crossing,) = call(across, [shape(ROWS + TAIL, width, BF16)], [late, late_rows, came, kept], ROWS * width)
    crossed = to_member(crossing, across_x)
    (image_grad,) = call(image_end, [shape(ROWS, width, F32)], [kept, *arrived], ROWS * width)
    text_grad_out, loss = call(
        text_end,
        [shape(ROWS, width, F32), shape(1, ROWS, F32)],
        [late, late_rows, came, crossed],
        ROWS * width,
    )
    return (image_grad, text_grad_out, loss.reshape(ROWS))


def solution(mesh):
    placed = (
        P(("blk", "grp"), None),
        P(("blk", "grp"), None),
        P(("blk", "grp"), None),
        P(("blk", "grp")),
        P("blk"),
        P(),
        P(),
        P(),
    )
    return jax.shard_map(
        on_device,
        mesh=mesh,
        in_specs=placed,
        out_specs=(P(("blk", "grp"), None), P(("blk", "grp"), None), P(("blk", "grp"))),
        check_vma=False,
    )
```

```python
import functools

import jax
import jax.numpy as jnp
from jax import lax
from jax.experimental import pallas as pl
from jax.experimental.pallas import tpu as pltpu
from jax.sharding import PartitionSpec as P


NBLK = 32
XH, Y, CORE = 2, 4, 2
ROWS = 112
SETS = Y * ROWS
SPAN = XH * Y * CORE * ROWS
TAIL = 16
LOG2E = 1.4426950408889634
LN2 = 0.6931471805599453
CHUNK = 32
Y_ORDER = (1, 3, 2)
F32 = jnp.float32
BF16 = jnp.bfloat16


def spot(xh, y, core):
    return (xh * Y + y) * CORE + core


def member_route(move):
    return [
        (spot(xh, y, c), spot(*move(xh, y, c)))
        for xh in range(XH)
        for y in range(Y)
        for c in range(CORE)
    ]


def across_x(xh, y, c):
    return (1 - xh, y, c)


def across_core(xh, y, c):
    return (xh, y, 1 - c)


def along_y(steps):
    return lambda xh, y, c: (xh, (y + steps) % Y, c)


def stay(xh, y, c):
    return (xh, y, c)


def to_member(block, move):
    return lax.ppermute(block, "grp", member_route(move))


def to_next_group(block, move):
    ngrp = XH * Y * CORE
    route = [
        (b * ngrp + s, ((b + 1) % NBLK) * ngrp + t)
        for b in range(NBLK)
        for s, t in member_route(move)
    ]
    return lax.ppermute(block, ("blk", "grp"), route)


def gather_y(block):
    groups = [[spot(xh, y, c) for y in range(Y)] for xh in range(XH) for c in range(CORE)]
    return lax.all_gather(block, "grp", axis_index_groups=groups, tiled=True)


VMEM = pl.BlockSpec(memory_space=pltpu.VMEM)
SMEM = pl.BlockSpec(memory_space=pltpu.SMEM)
HBM = pl.BlockSpec(memory_space=pltpu.HBM)


def call(body, outs, ins, flops, scratch=(), far=0):
    size = sum(x.size * x.dtype.itemsize for x in [*ins, *outs])
    ins = [
        pltpu.with_memory_space_constraint(x, pltpu.HBM) if i < far else x
        for i, x in enumerate(ins)
    ]
    return pl.pallas_call(
        body,
        out_shape=outs,
        in_specs=[HBM if i < far else SMEM if x.size == 1 else VMEM for i, x in enumerate(ins)],
        out_specs=[VMEM] * len(outs),
        scratch_shapes=list(scratch),
        cost_estimate=pl.CostEstimate(flops=flops, bytes_accessed=size, transcendentals=0),
        compiler_params=pltpu.CompilerParams(vmem_limit_bytes=12 * 1024 * 1024),
    )(*ins)


def shape(rows, cols, dtype):
    return jax.ShapeDtypeStruct((rows, cols), dtype)


def labels_of(match_ref, member, other):
    core = (member ^ other) & (CORE - 1)
    xh = member // (Y * CORE)
    lane = lax.broadcasted_iota(jnp.int32, (8, 128), 1)
    last = match_ref.shape[0] - 1
    tiles = []
    for q in range(-(-SETS // 128)):
        tile = jnp.zeros((8, 128), jnp.int32)
        for y in range(q * 128 // ROWS, min(Y - 1, (q * 128 + 127) // ROWS) + 1):
            shift = ROWS * (xh * Y * CORE + core + y)
            row = q + shift // 128
            turn = shift % 128
            pieces = []
            for r in (row, row + 1):
                piece = match_ref[pl.ds(jnp.minimum(r, last), 1), :]
                piece = jnp.broadcast_to(piece, (8, 128))
                pieces.append(pltpu.roll(piece, (128 - turn) % 128, 1))
            found = jnp.where(lane < 128 - turn, pieces[0], pieces[1])
            here = q * 128 + lane
            tile = jnp.where((here >= y * ROWS) & (here < (y + 1) * ROWS), found, tile)
        tiles.append(tile)
    return jnp.concatenate(tiles, axis=1)[0:1, :SETS]


def weigh(s_ref, labels, place, step, scale, bias, w_ref, lost_ref, first):
    here, member = place
    factor, offset = scale * LOG2E, bias * LOG2E
    turned = (here - step) & (NBLK - 1)
    behind = (turned - 1) & (NBLK - 1)
    partner = member ^ (Y * CORE)
    bases = [
        turned * SPAN + member * ROWS,
        turned * SPAN + partner * ROWS - ROWS,
        behind * SPAN + member * ROWS - 2 * ROWS,
        behind * SPAN + partner * ROWS - 3 * ROWS,
    ]

    def chunk(i, carry):
        start = pl.multiple_of(i * CHUNK, CHUNK)
        rows = start + lax.broadcasted_iota(jnp.int32, (CHUNK, 1), 0)
        base = jnp.where(
            rows < 2 * ROWS,
            jnp.where(rows < ROWS, bases[0], bases[1]),
            jnp.where(rows < 3 * ROWS, bases[2], bases[3]),
        )
        logits = factor * s_ref[pl.ds(start, CHUNK), :] + offset
        paired = (rows + base) == labels
        t = jnp.where(paired, -logits, logits)
        e = jnp.exp2(-jnp.abs(t))
        more = jnp.where(e < 1e-4, LOG2E * e, jnp.log2(1.0 + e))
        lost = jnp.maximum(t, 0.0) + more
        sig = jnp.exp2(t - lost)
        w_ref[pl.ds(start, CHUNK), :] = jnp.where(paired, -sig, sig).astype(BF16)
        total = jnp.sum(lost, axis=1, keepdims=True)
        if not first:
            total = total + lost_ref[pl.ds(start, CHUNK), :]
        lost_ref[pl.ds(start, CHUNK), :] = total
        return carry

    lax.fori_loop(0, 2 * XH * ROWS // CHUNK, chunk, 0, unroll=True)


def logits_of(texts, images):
    return lax.dot_general(texts, images, (((1,), (1,)), ((), ())), preferred_element_type=F32)


def image_part(weights, texts):
    return lax.dot_general(weights, texts, (((0,), (0,)), ((), ())), preferred_element_type=F32)


def here_and_member():
    return lax.axis_index("blk"), lax.axis_index("grp")


def fetch(pairs, sems):
    copies = [pltpu.make_async_copy(a, b, sems.at[i]) for i, (a, b) in enumerate(pairs)]
    for copy in copies:
        copy.start()
    return copies


def first_half(
    match, t0, step, scale, bias, t1, t2, t3, images, texts, w, part, lost,
    s, match_v, sems,
):
    copies = fetch(
        [(t0, texts.at[:ROWS, :]), (match, match_v)], sems
    )
    for i, t in enumerate((t1, t2, t3)):
        texts[(i + 1) * ROWS : (i + 2) * ROWS, :] = t[...]
    copies[0].wait()
    s[...] = logits_of(texts[...], images[...])
    for copy in copies[1:]:
        copy.wait()
    place = here_and_member()
    labels = labels_of(match_v, place[1], 0)
    weigh(s, labels, place, step[0], scale[0], bias[0], w, lost, True)
    part[...] = jnp.dot(w[...], images[...], preferred_element_type=F32)


def row_of(column):
    r = lax.broadcasted_iota(jnp.int32, (ROWS, 128), 0)
    c = lax.broadcasted_iota(jnp.int32, (ROWS, 128), 1)
    return jnp.sum(jnp.where(r == c, column, 0.0), axis=0, keepdims=True)


def second_half(
    match, step, scale, bias, texts, images, part, lost, acc, loss_acc,
    w, sent, late_rows, s, lost_all, match_v, sems,
):
    copies = fetch([(match, match_v)], sems)
    s[...] = logits_of(texts[...], images[...])
    lost_all[...] = lost[...]
    for copy in copies:
        copy.wait()
    place = here_and_member()
    factor = scale[0]
    labels = labels_of(match_v, place[1], 1)
    weigh(s, labels, place, step[0], factor, bias[0], w, lost_all, False)
    grad = jnp.dot(w[: 2 * ROWS, :], images[...], preferred_element_type=F32)
    grad = factor * (grad + part[: 2 * ROWS, :])
    sent[:ROWS, :] = (acc[...] + grad[:ROWS]).astype(BF16)
    sent[ROWS : 2 * ROWS, :] = grad[ROWS:].astype(BF16)
    rows = [row_of(lost_all[i * ROWS : (i + 1) * ROWS, :]) * (LN2 / SPAN) for i in range(4)]
    at = lax.broadcasted_iota(jnp.int32, (TAIL, 128), 0)
    tail = jnp.where(at == 0, rows[0], jnp.where(at == 1, rows[1], 0.0))
    at = lax.broadcasted_iota(jnp.int32, (TAIL, ROWS), 0)
    tail = tail[:, :ROWS] + jnp.where(at == 0, loss_acc[...], 0.0)
    sent[2 * ROWS :, :] = jnp.zeros((TAIL, sent.shape[1]), BF16)
    sent[2 * ROWS :, :ROWS] = tail.astype(BF16)
    at = lax.broadcasted_iota(jnp.int32, (8, 128), 0)
    late_rows[...] = jnp.where(at == 0, rows[2], jnp.where(at == 1, rows[3], factor))


def image_other(late_rows, w, texts, out):
    out[...] = (late_rows[2:3, 0:1] * image_part(w[...], texts[...])).astype(BF16)


def rest(late_rows, w_own, w_other, texts, images, part, image_own, late):
    factor = late_rows[2:3, 0:1]
    image_own[...] = factor * image_part(w_own[...], texts[...])
    grad = jnp.dot(w_other[2 * ROWS :, :], images[...], preferred_element_type=F32)
    late[...] = factor * (grad + part[2 * ROWS :, :])


def image_sum(steps, own, came, *refs):
    y = (lax.axis_index("grp") // CORE) & (Y - 1)
    for step, out in zip(steps, refs[-len(steps) :]):
        start = pl.multiple_of(((y + step) & (Y - 1)) * ROWS, 16)
        rows = pl.ds(start, ROWS)
        out[...] = (own[rows, :] + came[rows, :].astype(F32)).astype(out.dtype)


def across(late, late_rows, came, token, sent):
    sent[:ROWS, :] = (late[ROWS:, :] + came[ROWS : 2 * ROWS, :].astype(F32)).astype(BF16)
    sent[ROWS:, :] = jnp.zeros((TAIL, sent.shape[1]), BF16)
    tail = came[2 * ROWS :, :128].astype(F32)
    sent[ROWS:, :128] = (tail[1:2, :] + late_rows[1:2, :] + jnp.zeros((TAIL, 128), F32)).astype(BF16)


def image_end(kept, one, two, three, out, token):
    token[...] = kept[:8, :128]
    out[...] = kept[...] + one[...].astype(F32) + two[...].astype(F32) + three[...].astype(F32)


def text_end(late, late_rows, came, crossed, token, grad, loss):
    grad[...] = late[:ROWS, :] + came[:ROWS, :].astype(F32) + crossed[:ROWS, :].astype(F32)
    ahead = came[2 * ROWS :, :128].astype(F32)
    beside = crossed[ROWS:, :128].astype(F32)
    loss[...] = (late_rows[0:1, :] + ahead[0:1, :] + beside[0:1, :])[:, :ROWS]


def on_device(image_emb, text_held, text_grad_acc, text_loss_acc, match, step, scale, bias):
    width = text_held.shape[1]

    text_z = to_next_group(text_held, stay)
    text_d = to_next_group(text_held, across_x)
    text_x = to_member(text_held, across_x)
    images = gather_y(image_emb)
    images_other = to_member(images, across_core)

    match = match.reshape(-1, 128)
    count = 2 * XH * ROWS
    big = 2 * count * SETS * width
    scratch = [
        pltpu.VMEM(match.shape, jnp.int32),
        pltpu.SemaphoreType.DMA((2,)),
    ]
    texts, w_own, part, lost = call(
        first_half,
        [shape(count, width, BF16), shape(count, SETS, BF16), shape(count, width, F32), shape(count, 1, F32)],
        [match, text_held, step, scale, bias, text_x, text_z, text_d, images],
        40 * big,
        [pltpu.VMEM((count, SETS), F32), *scratch],
        far=2,
    )
    w_other, ahead, late_rows = call(
        second_half,
        [shape(count, SETS, BF16), shape(2 * ROWS + TAIL, width, BF16), shape(8, 128, F32)],
        [match, step, scale, bias, texts, images_other, part, lost, text_grad_acc, text_loss_acc.reshape(1, ROWS)],
        2 * big,
        [pltpu.VMEM((count, SETS), F32), pltpu.VMEM((count, 1), F32), *scratch],
        far=1,
    )
    came = to_next_group(ahead, stay)
    (other,) = call(image_other, [shape(SETS, width, BF16)], [late_rows, w_other, texts], 20 * big)
    other_came = to_member(other, across_core)
    image_own, late = call(
        rest,
        [shape(SETS, width, F32), shape(2 * ROWS, width, F32)],
        [late_rows, w_own, w_other, texts, images_other, part],
        20 * big,
    )
    block = shape(ROWS, width, BF16)
    arrived = []
    token = ()
    for step_y in Y_ORDER:
        steps = (step_y,) if step_y != Y_ORDER[-1] else (step_y, 0)
        outs = [block, shape(ROWS, width, F32)][: len(steps)]
        sums = call(functools.partial(image_sum, steps), outs, [image_own, other_came, *token], 20 * big)
        arrived.append(to_member(sums[0], along_y(step_y)))
        token = sums[-1:]
    kept = token[0]
    (crossing,) = call(across, [shape(ROWS + TAIL, width, BF16)], [late, late_rows, came, kept], ROWS * width)
    crossed = to_member(crossing, across_x)
    image_grad, token = call(
        image_end, [shape(ROWS, width, F32), shape(8, 128, F32)], [kept, *arrived], 40 * big
    )
    text_grad_out, loss = call(
        text_end,
        [shape(ROWS, width, F32), shape(1, ROWS, F32)],
        [late, late_rows, came, crossed, token],
        ROWS * width,
    )
    return (image_grad, text_grad_out, loss.reshape(ROWS))


def solution(mesh):
    placed = (
        P(("blk", "grp"), None),
        P(("blk", "grp"), None),
        P(("blk", "grp"), None),
        P(("blk", "grp")),
        P("blk"),
        P(),
        P(),
        P(),
    )
    return jax.shard_map(
        on_device,
        mesh=mesh,
        in_specs=placed,
        out_specs=(P(("blk", "grp"), None), P(("blk", "grp"), None), P(("blk", "grp"))),
        check_vma=False,
    )
```

```python
import jax
import jax.numpy as jnp
from jax import lax
from jax.experimental import pallas as pl
from jax.experimental.pallas import tpu as pltpu
from jax.sharding import PartitionSpec as P


NBLK = 32
XH, Y, CORE = 2, 4, 2
ROWS = 112
SETS = Y * ROWS
LAG = XH * ROWS
SPAN = XH * Y * CORE * ROWS
TAIL = 16
LOG2E = 1.4426950408889634
LN2 = 0.6931471805599453
CHUNK = 32
F32 = jnp.float32
BF16 = jnp.bfloat16


def spot(xh, y, core):
    return (xh * Y + y) * CORE + core


def member_route(move):
    return [
        (spot(xh, y, c), spot(*move(xh, y, c)))
        for xh in range(XH)
        for y in range(Y)
        for c in range(CORE)
    ]


def across_x(xh, y, c):
    return (1 - xh, y, c)


def across_core(xh, y, c):
    return (xh, y, 1 - c)


def along_y(steps):
    return lambda xh, y, c: (xh, (y + steps) % Y, c)


def stay(xh, y, c):
    return (xh, y, c)


def to_member(block, move):
    return lax.ppermute(block, "grp", member_route(move))


def to_next_group(block, move):
    ngrp = XH * Y * CORE
    route = [
        (b * ngrp + s, ((b + 1) % NBLK) * ngrp + t)
        for b in range(NBLK)
        for s, t in member_route(move)
    ]
    return lax.ppermute(block, ("blk", "grp"), route)


def gather_y(block):
    groups = [[spot(xh, y, c) for y in range(Y)] for xh in range(XH) for c in range(CORE)]
    return lax.all_gather(block, "grp", axis_index_groups=groups, tiled=True)


VMEM = pl.BlockSpec(memory_space=pltpu.VMEM)
SMEM = pl.BlockSpec(memory_space=pltpu.SMEM)
HBM = pl.BlockSpec(memory_space=pltpu.HBM)


def call(body, outs, ins, flops, scratch=(), far=0):
    size = flops // 64
    ins = [
        pltpu.with_memory_space_constraint(x, pltpu.HBM) if i < far else x
        for i, x in enumerate(ins)
    ]
    return pl.pallas_call(
        body,
        out_shape=outs,
        in_specs=[HBM if i < far else SMEM if x.size == 1 else VMEM for i, x in enumerate(ins)],
        out_specs=[VMEM] * len(outs),
        scratch_shapes=list(scratch),
        cost_estimate=pl.CostEstimate(flops=flops, bytes_accessed=size, transcendentals=0),
        compiler_params=pltpu.CompilerParams(vmem_limit_bytes=12 * 1024 * 1024),
    )(*ins)


def shape(rows, cols, dtype):
    return jax.ShapeDtypeStruct((rows, cols), dtype)


def held(rows, cols, dtype):
    return pltpu.VMEM((rows, cols), dtype)


def labels_of(match_ref, member, other):
    core = (member ^ other) & (CORE - 1)
    xh = member // (Y * CORE)
    lane = lax.broadcasted_iota(jnp.int32, (8, 128), 1)
    last = match_ref.shape[0] - 1
    tiles = []
    for q in range(-(-SETS // 128)):
        tile = jnp.zeros((8, 128), jnp.int32)
        for y in range(q * 128 // ROWS, min(Y - 1, (q * 128 + 127) // ROWS) + 1):
            shift = ROWS * (xh * Y * CORE + core + y)
            row = q + shift // 128
            turn = shift % 128
            pieces = []
            for r in (row, row + 1):
                piece = match_ref[pl.ds(jnp.minimum(r, last), 1), :]
                piece = jnp.broadcast_to(piece, (8, 128))
                pieces.append(pltpu.roll(piece, (128 - turn) % 128, 1))
            found = jnp.where(lane < 128 - turn, pieces[0], pieces[1])
            here = q * 128 + lane
            tile = jnp.where((here >= y * ROWS) & (here < (y + 1) * ROWS), found, tile)
        tiles.append(tile)
    return jnp.concatenate(tiles, axis=1)[0:1, :SETS]


def weigh(lag, s_ref, labels, member, given, w_ref, lost_ref=None, first=True):
    factor, offset = given[0:1, 0:1] * LOG2E, given[0:1, 1:2] * LOG2E
    anchor = given[0:1, 2:3].astype(jnp.int32)
    turned = (anchor - lag) & (NBLK - 1)
    partner = member ^ (Y * CORE)
    bases = [turned * SPAN + member * ROWS, turned * SPAN + (partner - 1) * ROWS]

    def chunk(i, carry):
        start = pl.multiple_of(i * CHUNK, CHUNK)
        rows = start + lax.broadcasted_iota(jnp.int32, (CHUNK, 1), 0)
        base = jnp.where(rows < ROWS, bases[0], bases[1])
        logits = factor * s_ref[pl.ds(start, CHUNK), :] + offset
        paired = (rows + base) == labels
        t = jnp.where(paired, -logits, logits)
        e = jnp.exp2(-jnp.abs(t))
        more = jnp.where(e < 1e-4, LOG2E * e, jnp.log2(1.0 + e))
        lost = jnp.maximum(t, 0.0) + more
        sig = jnp.exp2(t - lost)
        w_ref[pl.ds(start, CHUNK), :] = jnp.where(paired, -sig, sig).astype(BF16)
        if lost_ref is not None:
            total = jnp.sum(lost, axis=1, keepdims=True)
            if not first:
                total = total + lost_ref[pl.ds(start, CHUNK), :]
            lost_ref[pl.ds(start, CHUNK), :] = total
        return carry

    lax.fori_loop(0, XH * ROWS // CHUNK, chunk, 0, unroll=True)


def logits_of(texts, images):
    return lax.dot_general(texts, images, (((1,), (1,)), ((), ())), preferred_element_type=F32)


def image_part(weights, texts):
    return lax.dot_general(weights, texts, (((0,), (0,)), ((), ())), preferred_element_type=F32)


def fetch(pairs, sems):
    copies = [pltpu.make_async_copy(a, b, sems.at[i]) for i, (a, b) in enumerate(pairs)]
    for copy in copies:
        copy.start()
    return copies


def own_logits(
    match, text, loss_hbm, given, t1, z, d, images, texts, s0, s1, labels, loss_acc, match_v, sems
):
    copies = fetch([(match, match_v), (text, texts.at[:ROWS, :]), (loss_hbm, loss_acc)], sems)
    for i, t in enumerate((t1, z, d)):
        texts[(i + 1) * ROWS : (i + 2) * ROWS, :] = t[...]
    s1[...] = logits_of(texts[LAG:, :], images[...])
    for copy in copies:
        copy.wait()
    s0[...] = logits_of(texts[:LAG, :], images[...])
    member = lax.axis_index("grp")
    at = lax.broadcasted_iota(jnp.int32, labels.shape, 0)
    labels[...] = jnp.where(at == 0, labels_of(match_v, member, 0), labels_of(match_v, member, 1))


def text_part(weights, halves):
    return sum(
        jnp.dot(w[...], x[...], preferred_element_type=F32) for w, x in zip(weights, halves)
    )


def row_of(column):
    r = lax.broadcasted_iota(jnp.int32, (ROWS, 128), 0)
    c = lax.broadcasted_iota(jnp.int32, (ROWS, 128), 1)
    return jnp.sum(jnp.where(r == c, column, 0.0), axis=0, keepdims=True)


def loss_rows(lost):
    rows = [row_of(lost[i * ROWS : (i + 1) * ROWS, :]) * (LN2 / SPAN) for i in range(XH)]
    at = lax.broadcasted_iota(jnp.int32, (TAIL, 128), 0)
    return jnp.where(at == 0, rows[0], jnp.where(at == 1, rows[1], 0.0))


def first_lag(
    given, labels, texts, s_own, own, other, acc, loss_acc, w_own, sent, s, w_other, lost
):
    member = lax.axis_index("grp")
    s[...] = logits_of(texts[:LAG, :], other[...])
    weigh(0, s_own, labels[0:1, :], member, given, w_own, lost, True)
    grad = jnp.dot(w_own[...], own[...], preferred_element_type=F32)
    weigh(0, s, labels[1:2, :], member, given, w_other, lost, False)
    grad = grad + jnp.dot(w_other[...], other[...], preferred_element_type=F32)
    grad = given[0:1, 0:1] * grad
    sent[:ROWS, :] = (acc[...] + grad[:ROWS]).astype(BF16)
    sent[ROWS : 2 * ROWS, :] = grad[ROWS:].astype(BF16)
    at = lax.broadcasted_iota(jnp.int32, (TAIL, ROWS), 0)
    tail = loss_rows(lost)[:, :ROWS] + jnp.where(at == 0, loss_acc[...], 0.0)
    sent[2 * ROWS :, :] = jnp.zeros((TAIL, sent.shape[1]), BF16)
    sent[2 * ROWS :, :ROWS] = tail.astype(BF16)


def image_parts(
    given, labels, w0, s1, texts, beside, own,
    w1, lost, kept, one, two, three, s_b, w, w_b, total,
):
    member = lax.axis_index("grp")
    there = member ^ 1
    row = labels[0:1, :]
    s_b[...] = logits_of(beside[...], own[...])
    weigh(1, s1, row, member, given, w1, lost, True)
    w[:LAG, :] = w0[...]
    w[LAG:, :] = w1[...]
    part = image_part(w[...], texts[...])
    weigh(0, s_b.at[:LAG, :], row, there, given, w_b.at[:LAG, :])
    weigh(1, s_b.at[LAG:, :], row, there, given, w_b.at[LAG:, :])
    part = part + image_part(w_b[...], beside[...])
    total[...] = given[0:1, 0:1] * part
    y = (member // CORE) & (Y - 1)
    for step, out in enumerate((kept, one, two, three)):
        start = pl.multiple_of(((y + step) & (Y - 1)) * ROWS, 16)
        out[...] = total[pl.ds(start, ROWS), :].astype(out.dtype)


def second_lag(
    given, labels, texts, w_own, lost_own, own, other, token, late, late_rows, s, w_other, lost
):
    member = lax.axis_index("grp")
    lost[...] = lost_own[...]
    s[...] = logits_of(texts[LAG:, :], other[...])
    weigh(1, s, labels[1:2, :], member, given, w_other, lost, False)
    late[...] = given[0:1, 0:1] * text_part((w_own, w_other), (own, other))
    late_rows[...] = loss_rows(lost)[:8, :]


def across(late, late_rows, came, sent):
    sent[:ROWS, :] = (late[ROWS:, :] + came[ROWS : 2 * ROWS, :].astype(F32)).astype(BF16)
    sent[ROWS:, :] = jnp.zeros((TAIL, sent.shape[1]), BF16)
    tail = came[2 * ROWS :, :128].astype(F32)
    sent[ROWS:, :128] = (tail[1:2, :] + late_rows[1:2, :] + jnp.zeros((TAIL, 128), F32)).astype(BF16)


def image_end(kept, one, two, three, out, token):
    token[...] = kept[:8, :128]
    out[...] = kept[...] + one[...].astype(F32) + two[...].astype(F32) + three[...].astype(F32)


def text_end(late, late_rows, came, crossed, token, grad, loss):
    grad[...] = late[:ROWS, :] + came[:ROWS, :].astype(F32) + crossed[:ROWS, :].astype(F32)
    ahead = came[2 * ROWS :, :128].astype(F32)
    beside = crossed[ROWS:, :128].astype(F32)
    loss[...] = (late_rows[0:1, :] + ahead[0:1, :] + beside[0:1, :])[:, :ROWS]


def on_device(image_emb, text_held, text_grad_acc, text_loss_acc, match, step, scale, bias):
    width = text_held.shape[1]

    text_z = to_next_group(text_held, stay)
    text_d = to_next_group(text_held, across_x)
    text_x = to_member(text_held, across_x)
    images = gather_y(image_emb)
    images_other = to_member(images, across_core)

    match = match.reshape(-1, 128)
    anchor = (lax.axis_index("blk").astype(jnp.int32) - step) & (NBLK - 1)
    given = jnp.concatenate([scale, bias, anchor.astype(F32), jnp.zeros((125,), F32)]).reshape(1, 128)

    big = 2 * LAG * SETS * width
    block = shape(ROWS, width, BF16)
    logits = held(LAG, SETS, F32)
    weights = held(LAG, SETS, BF16)
    texts, s0, s1, labels, loss_acc = call(
        own_logits,
        [shape(2 * LAG, width, BF16), logits, logits, held(8, SETS, jnp.int32), held(1, ROWS, F32)],
        [match, text_held, text_loss_acc.reshape(1, ROWS), given, text_x, text_z, text_d, images],
        2 * big,
        [pltpu.VMEM(match.shape, jnp.int32), pltpu.SemaphoreType.DMA((3,))],
        far=3,
    )
    texts_beside = to_member(texts, across_core)
    w0, ahead = call(
        first_lag,
        [weights, shape(LAG + TAIL, width, BF16)],
        [given, labels, texts, s0, images, images_other, text_grad_acc, loss_acc],
        3 * big,
        [logits, weights, held(LAG, 1, F32)],
    )
    came = to_next_group(ahead, stay)
    w1, lost1, kept, *sent = call(
        image_parts,
        [weights, held(LAG, 1, F32), held(ROWS, width, F32), block, block, block],
        [given, labels, w0, s1, texts, texts_beside, images],
        6 * big,
        [held(2 * LAG, SETS, F32), held(2 * LAG, SETS, BF16), held(2 * LAG, SETS, BF16), held(SETS, width, F32)],
    )
    arrived = [to_member(part, along_y(i + 1)) for i, part in enumerate(sent)]
    late, late_rows = call(
        second_lag,
        [held(LAG, width, F32), held(8, 128, F32)],
        [given, labels, texts, w1, lost1, images, images_other, kept],
        3 * big,
        [logits, weights, held(LAG, 1, F32)],
    )
    (crossing,) = call(across, [shape(ROWS + TAIL, width, BF16)], [late, late_rows, came], ROWS * width)
    crossed = to_member(crossing, across_x)
    image_grad, token = call(
        image_end, [shape(ROWS, width, F32), held(8, 128, F32)], [kept, *arrived], 40 * big
    )
    text_grad_out, loss = call(
        text_end,
        [shape(ROWS, width, F32), shape(1, ROWS, F32)],
        [late, late_rows, came, crossed, token],
        ROWS * width,
    )
    return (image_grad, text_grad_out, loss.reshape(ROWS))


def solution(mesh):
    placed = (
        P(("blk", "grp"), None),
        P(("blk", "grp"), None),
        P(("blk", "grp"), None),
        P(("blk", "grp")),
        P("blk"),
        P(),
        P(),
        P(),
    )
    return jax.shard_map(
        on_device,
        mesh=mesh,
        in_specs=placed,
        out_specs=(P(("blk", "grp"), None), P(("blk", "grp"), None), P(("blk", "grp"))),
        check_vma=False,
    )
```

```python
import jax
import jax.numpy as jnp
from jax import lax
from jax.experimental import pallas as pl
from jax.experimental.pallas import tpu as pltpu
from jax.sharding import PartitionSpec as P


NBLK = 32
XH, Y, CORE = 2, 4, 2
ROWS = 112
SETS = Y * ROWS
LAG = XH * ROWS
SPAN = XH * Y * CORE * ROWS
TAIL = 16
LOG2E = 1.4426950408889634
LN2 = 0.6931471805599453
CHUNK = 32
F32 = jnp.float32
BF16 = jnp.bfloat16


def spot(xh, y, core):
    return (xh * Y + y) * CORE + core


def member_route(move):
    return [
        (spot(xh, y, c), spot(*move(xh, y, c)))
        for xh in range(XH)
        for y in range(Y)
        for c in range(CORE)
    ]


def across_x(xh, y, c):
    return (1 - xh, y, c)


def across_core(xh, y, c):
    return (xh, y, 1 - c)


def along_y(steps):
    return lambda xh, y, c: (xh, (y + steps) % Y, c)


def stay(xh, y, c):
    return (xh, y, c)


def to_member(block, move):
    return lax.ppermute(block, "grp", member_route(move))


def to_next_group(block, move):
    ngrp = XH * Y * CORE
    route = [
        (b * ngrp + s, ((b + 1) % NBLK) * ngrp + t)
        for b in range(NBLK)
        for s, t in member_route(move)
    ]
    return lax.ppermute(block, ("blk", "grp"), route)


def gather_y(block):
    groups = [[spot(xh, y, c) for y in range(Y)] for xh in range(XH) for c in range(CORE)]
    return lax.all_gather(block, "grp", axis_index_groups=groups, tiled=True)


VMEM = pl.BlockSpec(memory_space=pltpu.VMEM)
SMEM = pl.BlockSpec(memory_space=pltpu.SMEM)
HBM = pl.BlockSpec(memory_space=pltpu.HBM)


def call(body, outs, ins, flops, scratch=(), far=0):
    size = flops // 64
    ins = [
        pltpu.with_memory_space_constraint(x, pltpu.HBM) if i < far else x
        for i, x in enumerate(ins)
    ]
    return pl.pallas_call(
        body,
        out_shape=outs,
        in_specs=[HBM if i < far else SMEM if x.size == 1 else VMEM for i, x in enumerate(ins)],
        out_specs=[VMEM] * len(outs),
        scratch_shapes=list(scratch),
        cost_estimate=pl.CostEstimate(flops=flops, bytes_accessed=size, transcendentals=0),
        compiler_params=pltpu.CompilerParams(vmem_limit_bytes=12 * 1024 * 1024),
    )(*ins)


def shape(rows, cols, dtype):
    return jax.ShapeDtypeStruct((rows, cols), dtype)


def held(rows, cols, dtype):
    return pltpu.VMEM((rows, cols), dtype)


def labels_of(match_ref, member, other):
    core = (member ^ other) & (CORE - 1)
    xh = member // (Y * CORE)
    lane = lax.broadcasted_iota(jnp.int32, (8, 128), 1)
    last = match_ref.shape[0] - 1
    tiles = []
    for q in range(-(-SETS // 128)):
        tile = jnp.zeros((8, 128), jnp.int32)
        for y in range(q * 128 // ROWS, min(Y - 1, (q * 128 + 127) // ROWS) + 1):
            shift = ROWS * (xh * Y * CORE + core + y)
            row = q + shift // 128
            turn = shift % 128
            pieces = []
            for r in (row, row + 1):
                piece = match_ref[pl.ds(jnp.minimum(r, last), 1), :]
                piece = jnp.broadcast_to(piece, (8, 128))
                pieces.append(pltpu.roll(piece, (128 - turn) % 128, 1))
            found = jnp.where(lane < 128 - turn, pieces[0], pieces[1])
            here = q * 128 + lane
            tile = jnp.where((here >= y * ROWS) & (here < (y + 1) * ROWS), found, tile)
        tiles.append(tile)
    return jnp.concatenate(tiles, axis=1)[0:1, :SETS]


def weigh(lag, s_ref, labels, member, given, w_ref, lost_ref=None, first=True):
    factor, offset = given[0:1, 0:1] * LOG2E, given[0:1, 1:2] * LOG2E
    anchor = given[0:1, 2:3].astype(jnp.int32)
    turned = (anchor - lag) & (NBLK - 1)
    partner = member ^ (Y * CORE)
    bases = [turned * SPAN + member * ROWS, turned * SPAN + (partner - 1) * ROWS]

    def chunk(i, carry):
        start = pl.multiple_of(i * CHUNK, CHUNK)
        rows = start + lax.broadcasted_iota(jnp.int32, (CHUNK, 1), 0)
        base = jnp.where(rows < ROWS, bases[0], bases[1])
        logits = factor * s_ref[pl.ds(start, CHUNK), :] + offset
        paired = (rows + base) == labels
        t = jnp.where(paired, -logits, logits)
        e = jnp.exp2(-jnp.abs(t))
        more = jnp.where(e < 1e-4, LOG2E * e, jnp.log2(1.0 + e))
        lost = jnp.maximum(t, 0.0) + more
        sig = jnp.exp2(t - lost)
        w_ref[pl.ds(start, CHUNK), :] = jnp.where(paired, -sig, sig).astype(BF16)
        if lost_ref is not None:
            total = jnp.sum(lost, axis=1, keepdims=True)
            if not first:
                total = total + lost_ref[pl.ds(start, CHUNK), :]
            lost_ref[pl.ds(start, CHUNK), :] = total
        return carry

    lax.fori_loop(0, XH * ROWS // CHUNK, chunk, 0, unroll=True)


def logits_of(texts, images):
    return lax.dot_general(texts, images, (((1,), (1,)), ((), ())), preferred_element_type=F32)


def image_part(weights, texts):
    return lax.dot_general(weights, texts, (((0,), (0,)), ((), ())), preferred_element_type=F32)


def fetch(pairs, sems):
    copies = [pltpu.make_async_copy(a, b, sems.at[i]) for i, (a, b) in enumerate(pairs)]
    for copy in copies:
        copy.start()
    return copies


def own_logits(
    match, text, loss_hbm, given, t1, images, texts, s0, labels, loss_acc, match_v, sems
):
    copies = fetch([(match, match_v), (text, texts.at[:ROWS, :]), (loss_hbm, loss_acc)], sems)
    texts[ROWS:, :] = t1[...]
    for copy in copies:
        copy.wait()
    s0[...] = logits_of(texts[...], images[...])
    member = lax.axis_index("grp")
    at = lax.broadcasted_iota(jnp.int32, labels.shape, 0)
    labels[...] = jnp.where(at == 0, labels_of(match_v, member, 0), labels_of(match_v, member, 1))


def late_texts(texts0, z, d, texts):
    texts[:LAG, :] = texts0[...]
    texts[LAG : LAG + ROWS, :] = z[...]
    texts[LAG + ROWS :, :] = d[...]


def row_of(column):
    r = lax.broadcasted_iota(jnp.int32, (ROWS, 128), 0)
    c = lax.broadcasted_iota(jnp.int32, (ROWS, 128), 1)
    return jnp.sum(jnp.where(r == c, column, 0.0), axis=0, keepdims=True)


def loss_rows(lost):
    rows = [row_of(lost[i * ROWS : (i + 1) * ROWS, :]) * (LN2 / SPAN) for i in range(XH)]
    at = lax.broadcasted_iota(jnp.int32, (TAIL, 128), 0)
    return jnp.where(at == 0, rows[0], jnp.where(at == 1, rows[1], 0.0))


def first_lag(
    given, labels, texts, s_own, own, other, acc, loss_acc, w_own, sent, s, w_other, lost
):
    member = lax.axis_index("grp")
    s[...] = logits_of(texts[...], other[...])
    weigh(0, s_own, labels[0:1, :], member, given, w_own, lost, True)
    grad = jnp.dot(w_own[...], own[...], preferred_element_type=F32)
    weigh(0, s, labels[1:2, :], member, given, w_other, lost, False)
    grad = grad + jnp.dot(w_other[...], other[...], preferred_element_type=F32)
    grad = given[0:1, 0:1] * grad
    sent[:ROWS, :] = (acc[...] + grad[:ROWS]).astype(BF16)
    sent[ROWS : 2 * ROWS, :] = grad[ROWS:].astype(BF16)
    at = lax.broadcasted_iota(jnp.int32, (TAIL, ROWS), 0)
    tail = loss_rows(lost)[:, :ROWS] + jnp.where(at == 0, loss_acc[...], 0.0)
    sent[2 * ROWS :, :] = jnp.zeros((TAIL, sent.shape[1]), BF16)
    sent[2 * ROWS :, :ROWS] = tail.astype(BF16)


def second_lag(
    given, labels, texts, own, other, w_own, late, late_rows, s_own, s, w_other, lost
):
    member = lax.axis_index("grp")
    s_own[...] = logits_of(texts[LAG:, :], own[...])
    s[...] = logits_of(texts[LAG:, :], other[...])
    weigh(1, s_own, labels[0:1, :], member, given, w_own, lost, True)
    grad = jnp.dot(w_own[...], own[...], preferred_element_type=F32)
    weigh(1, s, labels[1:2, :], member, given, w_other, lost, False)
    grad = grad + jnp.dot(w_other[...], other[...], preferred_element_type=F32)
    late[...] = given[0:1, 0:1] * grad
    late_rows[...] = loss_rows(lost)[:8, :]


def image_parts(
    given, labels, w0, w1, texts, beside, own, token, kept, one, two, three, s_b, w, w_b, total
):
    member = lax.axis_index("grp")
    there = member ^ 1
    row = labels[0:1, :]
    s_b[...] = logits_of(beside[...], own[...])
    w[:LAG, :] = w0[...]
    w[LAG:, :] = w1[...]
    weigh(0, s_b.at[:LAG, :], row, there, given, w_b.at[:LAG, :])
    weigh(1, s_b.at[LAG:, :], row, there, given, w_b.at[LAG:, :])
    part = image_part(w[...], texts[...]) + image_part(w_b[...], beside[...])
    total[...] = given[0:1, 0:1] * part
    y = (member // CORE) & (Y - 1)
    for step, out in enumerate((kept, one, two, three)):
        start = pl.multiple_of(((y + step) & (Y - 1)) * ROWS, 16)
        out[...] = total[pl.ds(start, ROWS), :].astype(out.dtype)


def across(late, late_rows, came, sent):
    sent[:ROWS, :] = (late[ROWS:, :] + came[ROWS : 2 * ROWS, :].astype(F32)).astype(BF16)
    sent[ROWS:, :] = jnp.zeros((TAIL, sent.shape[1]), BF16)
    tail = came[2 * ROWS :, :128].astype(F32)
    sent[ROWS:, :128] = (tail[1:2, :] + late_rows[1:2, :] + jnp.zeros((TAIL, 128), F32)).astype(BF16)


def image_end(kept, one, two, three, out, token):
    token[...] = kept[:8, :128]
    out[...] = kept[...] + one[...].astype(F32) + two[...].astype(F32) + three[...].astype(F32)


def text_end(late, late_rows, came, crossed, token, grad, loss):
    grad[...] = late[:ROWS, :] + came[:ROWS, :].astype(F32) + crossed[:ROWS, :].astype(F32)
    ahead = came[2 * ROWS :, :128].astype(F32)
    beside = crossed[ROWS:, :128].astype(F32)
    loss[...] = (late_rows[0:1, :] + ahead[0:1, :] + beside[0:1, :])[:, :ROWS]


def on_device(image_emb, text_held, text_grad_acc, text_loss_acc, match, step, scale, bias):
    width = text_held.shape[1]

    text_z = to_next_group(text_held, stay)
    text_d = to_next_group(text_held, across_x)
    text_x = to_member(text_held, across_x)
    images = gather_y(image_emb)
    images_other = to_member(images, across_core)

    match = match.reshape(-1, 128)
    anchor = (lax.axis_index("blk").astype(jnp.int32) - step) & (NBLK - 1)
    given = jnp.concatenate([scale, bias, anchor.astype(F32), jnp.zeros((125,), F32)]).reshape(1, 128)

    big = 2 * LAG * SETS * width
    block = shape(ROWS, width, BF16)
    logits = held(LAG, SETS, F32)
    weights = held(LAG, SETS, BF16)
    texts0, s0, labels, loss_acc = call(
        own_logits,
        [shape(LAG, width, BF16), logits, held(8, SETS, jnp.int32), held(1, ROWS, F32)],
        [match, text_held, text_loss_acc.reshape(1, ROWS), given, text_x, images],
        2 * big,
        [pltpu.VMEM(match.shape, jnp.int32), pltpu.SemaphoreType.DMA((3,))],
        far=3,
    )
    w0, ahead = call(
        first_lag,
        [weights, shape(LAG + TAIL, width, BF16)],
        [given, labels, texts0, s0, images, images_other, text_grad_acc, loss_acc],
        3 * big,
        [logits, weights, held(LAG, 1, F32)],
    )
    came = to_next_group(ahead, stay)
    (texts,) = call(late_texts, [shape(2 * LAG, width, BF16)], [texts0, text_z, text_d], big // 8)
    texts_beside = to_member(texts, across_core)
    w1, late, late_rows = call(
        second_lag,
        [weights, held(LAG, width, F32), held(8, 128, F32)],
        [given, labels, texts, images, images_other],
        4 * big,
        [logits, logits, weights, held(LAG, 1, F32)],
    )
    kept, *sent = call(
        image_parts,
        [held(ROWS, width, F32), block, block, block],
        [given, labels, w0, w1, texts, texts_beside, images, late_rows],
        6 * big,
        [held(2 * LAG, SETS, F32), held(2 * LAG, SETS, BF16), held(2 * LAG, SETS, BF16), held(SETS, width, F32)],
    )
    arrived = [to_member(part, along_y(i + 1)) for i, part in enumerate(sent)]
    (crossing,) = call(across, [shape(ROWS + TAIL, width, BF16)], [late, late_rows, came], ROWS * width)
    crossed = to_member(crossing, across_x)
    image_grad, token = call(
        image_end, [shape(ROWS, width, F32), held(8, 128, F32)], [kept, *arrived], 40 * big
    )
    text_grad_out, loss = call(
        text_end,
        [shape(ROWS, width, F32), shape(1, ROWS, F32)],
        [late, late_rows, came, crossed, token],
        ROWS * width,
    )
    return (image_grad, text_grad_out, loss.reshape(ROWS))


def solution(mesh):
    placed = (
        P(("blk", "grp"), None),
        P(("blk", "grp"), None),
        P(("blk", "grp"), None),
        P(("blk", "grp")),
        P("blk"),
        P(),
        P(),
        P(),
    )
    return jax.shard_map(
        on_device,
        mesh=mesh,
        in_specs=placed,
        out_specs=(P(("blk", "grp"), None), P(("blk", "grp"), None), P(("blk", "grp"))),
        check_vma=False,
    )
```

```python
import jax
import jax.numpy as jnp
from jax import lax
from jax.experimental import pallas as pl
from jax.experimental.pallas import tpu as pltpu
from jax.sharding import PartitionSpec as P


NBLK = 32
XH, Y, CORE = 2, 4, 2
ROWS = 112
SETS = Y * ROWS
LAG = XH * ROWS
SPAN = XH * Y * CORE * ROWS
TAIL = 16
LOG2E = 1.4426950408889634
LN2 = 0.6931471805599453
CHUNK = 32
F32 = jnp.float32
BF16 = jnp.bfloat16


def spot(xh, y, core):
    return (xh * Y + y) * CORE + core


def member_route(move):
    return [
        (spot(xh, y, c), spot(*move(xh, y, c)))
        for xh in range(XH)
        for y in range(Y)
        for c in range(CORE)
    ]


def across_x(xh, y, c):
    return (1 - xh, y, c)


def across_core(xh, y, c):
    return (xh, y, 1 - c)


def along_y(steps):
    return lambda xh, y, c: (xh, (y + steps) % Y, c)


def stay(xh, y, c):
    return (xh, y, c)


def to_member(block, move):
    return lax.ppermute(block, "grp", member_route(move))


def to_next_group(block, move):
    ngrp = XH * Y * CORE
    route = [
        (b * ngrp + s, ((b + 1) % NBLK) * ngrp + t)
        for b in range(NBLK)
        for s, t in member_route(move)
    ]
    return lax.ppermute(block, ("blk", "grp"), route)


def gather_y(block):
    groups = [[spot(xh, y, c) for y in range(Y)] for xh in range(XH) for c in range(CORE)]
    return lax.all_gather(block, "grp", axis_index_groups=groups, tiled=True)


VMEM = pl.BlockSpec(memory_space=pltpu.VMEM)
SMEM = pl.BlockSpec(memory_space=pltpu.SMEM)
HBM = pl.BlockSpec(memory_space=pltpu.HBM)


def call(body, outs, ins, flops, scratch=(), far=0):
    size = flops // 64
    ins = [
        pltpu.with_memory_space_constraint(x, pltpu.HBM) if i < far else x
        for i, x in enumerate(ins)
    ]
    return pl.pallas_call(
        body,
        out_shape=outs,
        in_specs=[HBM if i < far else SMEM if x.size == 1 else VMEM for i, x in enumerate(ins)],
        out_specs=[VMEM] * len(outs),
        scratch_shapes=list(scratch),
        cost_estimate=pl.CostEstimate(flops=flops, bytes_accessed=size, transcendentals=0),
        compiler_params=pltpu.CompilerParams(vmem_limit_bytes=12 * 1024 * 1024),
    )(*ins)


def shape(rows, cols, dtype):
    return jax.ShapeDtypeStruct((rows, cols), dtype)


def held(rows, cols, dtype):
    return pltpu.VMEM((rows, cols), dtype)


def labels_of(match_ref, member, other):
    core = (member ^ other) & (CORE - 1)
    xh = member // (Y * CORE)
    lane = lax.broadcasted_iota(jnp.int32, (8, 128), 1)
    last = match_ref.shape[0] - 1
    tiles = []
    for q in range(-(-SETS // 128)):
        tile = jnp.zeros((8, 128), jnp.int32)
        for y in range(q * 128 // ROWS, min(Y - 1, (q * 128 + 127) // ROWS) + 1):
            shift = ROWS * (xh * Y * CORE + core + y)
            row = q + shift // 128
            turn = shift % 128
            pieces = []
            for r in (row, row + 1):
                piece = match_ref[pl.ds(jnp.minimum(r, last), 1), :]
                piece = jnp.broadcast_to(piece, (8, 128))
                pieces.append(pltpu.roll(piece, (128 - turn) % 128, 1))
            found = jnp.where(lane < 128 - turn, pieces[0], pieces[1])
            here = q * 128 + lane
            tile = jnp.where((here >= y * ROWS) & (here < (y + 1) * ROWS), found, tile)
        tiles.append(tile)
    return jnp.concatenate(tiles, axis=1)[0:1, :SETS]


def weigh(lag, s_ref, labels, member, given, w_ref, lost_ref=None, first=True):
    factor, offset = given[0:1, 0:1] * LOG2E, given[0:1, 1:2] * LOG2E
    anchor = given[0:1, 2:3].astype(jnp.int32)
    turned = (anchor - lag) & (NBLK - 1)
    partner = member ^ (Y * CORE)
    bases = [turned * SPAN + member * ROWS, turned * SPAN + (partner - 1) * ROWS]

    def chunk(i, carry):
        start = pl.multiple_of(i * CHUNK, CHUNK)
        rows = start + lax.broadcasted_iota(jnp.int32, (CHUNK, 1), 0)
        base = jnp.where(rows < ROWS, bases[0], bases[1])
        logits = factor * s_ref[pl.ds(start, CHUNK), :] + offset
        paired = (rows + base) == labels
        t = jnp.where(paired, -logits, logits)
        e = jnp.exp2(-jnp.abs(t))
        more = jnp.where(e < 1e-4, LOG2E * e * (1.0 - 0.5 * e), jnp.log2(1.0 + e))
        lost = jnp.maximum(t, 0.0) + more
        sig = jnp.exp2(t - lost)
        w_ref[pl.ds(start, CHUNK), :] = jnp.where(paired, -sig, sig).astype(BF16)
        if lost_ref is not None:
            total = jnp.sum(lost, axis=1, keepdims=True)
            if not first:
                total = total + lost_ref[pl.ds(start, CHUNK), :]
            lost_ref[pl.ds(start, CHUNK), :] = total
        return carry

    lax.fori_loop(0, XH * ROWS // CHUNK, chunk, 0, unroll=True)


def logits_of(texts, images):
    return lax.dot_general(texts, images, (((1,), (1,)), ((), ())), preferred_element_type=F32)


def image_part(weights, texts):
    return lax.dot_general(weights, texts, (((0,), (0,)), ((), ())), preferred_element_type=F32)


def fetch(pairs, sems):
    copies = [pltpu.make_async_copy(a, b, sems.at[i]) for i, (a, b) in enumerate(pairs)]
    for copy in copies:
        copy.start()
    return copies


def own_logits(
    match, text, loss_hbm, given, t1, images, texts, s0, labels, loss_acc, match_v, sems
):
    copies = fetch([(match, match_v), (text, texts.at[:ROWS, :]), (loss_hbm, loss_acc)], sems)
    texts[ROWS:, :] = t1[...]
    for copy in copies:
        copy.wait()
    s0[...] = logits_of(texts[...], images[...])
    member = lax.axis_index("grp")
    at = lax.broadcasted_iota(jnp.int32, labels.shape, 0)
    labels[...] = jnp.where(at == 0, labels_of(match_v, member, 0), labels_of(match_v, member, 1))


def late_texts(texts0, z, d, texts):
    texts[:LAG, :] = texts0[...]
    texts[LAG : LAG + ROWS, :] = z[...]
    texts[LAG + ROWS :, :] = d[...]


def row_of(column):
    r = lax.broadcasted_iota(jnp.int32, (ROWS, 128), 0)
    c = lax.broadcasted_iota(jnp.int32, (ROWS, 128), 1)
    return jnp.sum(jnp.where(r == c, column, 0.0), axis=0, keepdims=True)


def loss_rows(lost):
    rows = [row_of(lost[i * ROWS : (i + 1) * ROWS, :]) * (LN2 / SPAN) for i in range(XH)]
    at = lax.broadcasted_iota(jnp.int32, (TAIL, 128), 0)
    return jnp.where(at == 0, rows[0], jnp.where(at == 1, rows[1], 0.0))


def first_lag(
    given, labels, texts, s_own, own, other, acc, loss_acc, w_own, sent, s, w_other, lost
):
    member = lax.axis_index("grp")
    s[...] = logits_of(texts[...], other[...])
    weigh(0, s_own, labels[0:1, :], member, given, w_own, lost, True)
    grad = jnp.dot(w_own[...], own[...], preferred_element_type=F32)
    weigh(0, s, labels[1:2, :], member, given, w_other, lost, False)
    grad = grad + jnp.dot(w_other[...], other[...], preferred_element_type=F32)
    grad = given[0:1, 0:1] * grad
    sent[:ROWS, :] = (acc[...] + grad[:ROWS]).astype(BF16)
    sent[ROWS : 2 * ROWS, :] = grad[ROWS:].astype(BF16)
    at = lax.broadcasted_iota(jnp.int32, (TAIL, ROWS), 0)
    tail = loss_rows(lost)[:, :ROWS] + jnp.where(at == 0, loss_acc[...], 0.0)
    sent[2 * ROWS :, :] = jnp.zeros((TAIL, sent.shape[1]), BF16)
    sent[2 * ROWS :, :ROWS] = tail.astype(BF16)


def second_lag(
    given, labels, texts, own, other, w_own, late, late_rows, s_own, s, w_other, lost
):
    member = lax.axis_index("grp")
    s_own[...] = logits_of(texts[LAG:, :], own[...])
    s[...] = logits_of(texts[LAG:, :], other[...])
    weigh(1, s_own, labels[0:1, :], member, given, w_own, lost, True)
    grad = jnp.dot(w_own[...], own[...], preferred_element_type=F32)
    weigh(1, s, labels[1:2, :], member, given, w_other, lost, False)
    grad = grad + jnp.dot(w_other[...], other[...], preferred_element_type=F32)
    late[...] = given[0:1, 0:1] * grad
    late_rows[...] = loss_rows(lost)[:8, :]


def image_parts(
    given, labels, w0, w1, texts, beside, own, token, kept, one, two, three, s_b, w, w_b, total
):
    member = lax.axis_index("grp")
    there = member ^ 1
    row = labels[0:1, :]
    s_b[...] = logits_of(beside[...], own[...])
    w[:LAG, :] = w0[...]
    w[LAG:, :] = w1[...]
    total[...] = image_part(w[...], texts[...])
    weigh(0, s_b.at[:LAG, :], row, there, given, w_b.at[:LAG, :])
    weigh(1, s_b.at[LAG:, :], row, there, given, w_b.at[LAG:, :])
    total[...] += image_part(w_b[...], beside[...])
    factor = given[0:1, 0:1]
    y = (member // CORE) & (Y - 1)
    for step, out in enumerate((kept, one, two, three)):
        start = pl.multiple_of(((y + step) & (Y - 1)) * ROWS, 16)
        out[...] = (factor * total[pl.ds(start, ROWS), :]).astype(out.dtype)


def across(late, late_rows, came, sent):
    sent[:ROWS, :] = (late[ROWS:, :] + came[ROWS : 2 * ROWS, :].astype(F32)).astype(BF16)
    sent[ROWS:, :] = jnp.zeros((TAIL, sent.shape[1]), BF16)
    tail = came[2 * ROWS :, :128].astype(F32)
    sent[ROWS:, :128] = (tail[1:2, :] + late_rows[1:2, :] + jnp.zeros((TAIL, 128), F32)).astype(BF16)


def image_end(kept, one, two, three, out, token):
    token[...] = kept[:8, :128]
    out[...] = kept[...] + one[...].astype(F32) + two[...].astype(F32) + three[...].astype(F32)


def text_end(late, late_rows, came, crossed, token, grad, loss):
    grad[...] = late[:ROWS, :] + came[:ROWS, :].astype(F32) + crossed[:ROWS, :].astype(F32)
    ahead = came[2 * ROWS :, :128].astype(F32)
    beside = crossed[ROWS:, :128].astype(F32)
    loss[...] = (late_rows[0:1, :] + ahead[0:1, :] + beside[0:1, :])[:, :ROWS]


def on_device(image_emb, text_held, text_grad_acc, text_loss_acc, match, step, scale, bias):
    width = text_held.shape[1]

    text_z = to_next_group(text_held, stay)
    text_d = to_next_group(text_held, across_x)
    text_x = to_member(text_held, across_x)
    images = gather_y(image_emb)
    images_other = to_member(images, across_core)

    match = match.reshape(-1, 128)
    anchor = (lax.axis_index("blk").astype(jnp.int32) - step) & (NBLK - 1)
    given = jnp.concatenate([scale, bias, anchor.astype(F32), jnp.zeros((125,), F32)]).reshape(1, 128)

    big = 2 * LAG * SETS * width
    block = shape(ROWS, width, BF16)
    logits = held(LAG, SETS, F32)
    weights = held(LAG, SETS, BF16)
    texts0, s0, labels, loss_acc = call(
        own_logits,
        [shape(LAG, width, BF16), logits, held(8, SETS, jnp.int32), held(1, ROWS, F32)],
        [match, text_held, text_loss_acc.reshape(1, ROWS), given, text_x, images],
        2 * big,
        [pltpu.VMEM(match.shape, jnp.int32), pltpu.SemaphoreType.DMA((3,))],
        far=3,
    )
    w0, ahead = call(
        first_lag,
        [weights, shape(LAG + TAIL, width, BF16)],
        [given, labels, texts0, s0, images, images_other, text_grad_acc, loss_acc],
        3 * big,
        [logits, weights, held(LAG, 1, F32)],
    )
    came = to_next_group(ahead, stay)
    (texts,) = call(late_texts, [shape(2 * LAG, width, BF16)], [texts0, text_z, text_d], big // 8)
    texts_beside = to_member(texts, across_core)
    w1, late, late_rows = call(
        second_lag,
        [weights, held(LAG, width, F32), held(8, 128, F32)],
        [given, labels, texts, images, images_other],
        4 * big,
        [logits, logits, weights, held(LAG, 1, F32)],
    )
    kept, *sent = call(
        image_parts,
        [held(ROWS, width, F32), block, block, block],
        [given, labels, w0, w1, texts, texts_beside, images, late_rows],
        6 * big,
        [held(2 * LAG, SETS, F32), held(2 * LAG, SETS, BF16), held(2 * LAG, SETS, BF16), held(SETS, width, F32)],
    )
    arrived = [to_member(part, along_y(i + 1)) for i, part in enumerate(sent)]
    (crossing,) = call(across, [shape(ROWS + TAIL, width, BF16)], [late, late_rows, came], ROWS * width)
    crossed = to_member(crossing, across_x)
    image_grad, token = call(
        image_end, [shape(ROWS, width, F32), held(8, 128, F32)], [kept, *arrived], 40 * big
    )
    text_grad_out, loss = call(
        text_end,
        [shape(ROWS, width, F32), shape(1, ROWS, F32)],
        [late, late_rows, came, crossed, token],
        ROWS * width,
    )
    return (image_grad, text_grad_out, loss.reshape(ROWS))


def solution(mesh):
    placed = (
        P(("blk", "grp"), None),
        P(("blk", "grp"), None),
        P(("blk", "grp"), None),
        P(("blk", "grp")),
        P("blk"),
        P(),
        P(),
        P(),
    )
    return jax.shard_map(
        on_device,
        mesh=mesh,
        in_specs=placed,
        out_specs=(P(("blk", "grp"), None), P(("blk", "grp"), None), P(("blk", "grp"))),
        check_vma=False,
    )
```

```python
import jax
import jax.numpy as jnp
from jax import lax
from jax.experimental import pallas as pl
from jax.experimental.pallas import tpu as pltpu
from jax.sharding import PartitionSpec as P


NBLK = 32
XH, Y, CORE = 2, 4, 2
ROWS = 112
SETS = Y * ROWS
LAG = XH * ROWS
SPAN = XH * Y * CORE * ROWS
TAIL = 16
STEPS = (0, 2, 1, 3)
LOG2E = 1.4426950408889634
LN2 = 0.6931471805599453
CHUNK = 32
F32 = jnp.float32
BF16 = jnp.bfloat16


def spot(xh, y, core):
    return (xh * Y + y) * CORE + core


def member_route(move):
    return [
        (spot(xh, y, c), spot(*move(xh, y, c)))
        for xh in range(XH)
        for y in range(Y)
        for c in range(CORE)
    ]


def across_x(xh, y, c):
    return (1 - xh, y, c)


def across_core(xh, y, c):
    return (xh, y, 1 - c)


def along_y(steps):
    return lambda xh, y, c: (xh, (y + steps) % Y, c)


def stay(xh, y, c):
    return (xh, y, c)


def to_member(block, move):
    return lax.ppermute(block, "grp", member_route(move))


def to_next_group(block, move):
    ngrp = XH * Y * CORE
    route = [
        (b * ngrp + s, ((b + 1) % NBLK) * ngrp + t)
        for b in range(NBLK)
        for s, t in member_route(move)
    ]
    return lax.ppermute(block, ("blk", "grp"), route)


def gather_y(block):
    groups = [[spot(xh, y, c) for y in range(Y)] for xh in range(XH) for c in range(CORE)]
    return lax.all_gather(block, "grp", axis_index_groups=groups, tiled=True)


VMEM = pl.BlockSpec(memory_space=pltpu.VMEM)
SMEM = pl.BlockSpec(memory_space=pltpu.SMEM)
HBM = pl.BlockSpec(memory_space=pltpu.HBM)


def call(body, outs, ins, flops, scratch=(), far=0):
    size = flops // 64
    ins = [
        pltpu.with_memory_space_constraint(x, pltpu.HBM) if i < far else x
        for i, x in enumerate(ins)
    ]
    return pl.pallas_call(
        body,
        out_shape=outs,
        in_specs=[HBM if i < far else SMEM if x.size == 1 else VMEM for i, x in enumerate(ins)],
        out_specs=[VMEM] * len(outs),
        scratch_shapes=list(scratch),
        cost_estimate=pl.CostEstimate(flops=flops, bytes_accessed=size, transcendentals=0),
        compiler_params=pltpu.CompilerParams(vmem_limit_bytes=12 * 1024 * 1024),
    )(*ins)


def shape(rows, cols, dtype):
    return jax.ShapeDtypeStruct((rows, cols), dtype)


def held(rows, cols, dtype):
    return pltpu.VMEM((rows, cols), dtype)


def labels_of(match_ref, member, other):
    core = (member ^ other) & (CORE - 1)
    xh = member // (Y * CORE)
    lane = lax.broadcasted_iota(jnp.int32, (8, 128), 1)
    last = match_ref.shape[0] - 1
    tiles = []
    for q in range(-(-SETS // 128)):
        tile = jnp.zeros((8, 128), jnp.int32)
        for y in range(q * 128 // ROWS, min(Y - 1, (q * 128 + 127) // ROWS) + 1):
            shift = ROWS * (xh * Y * CORE + core + y)
            row = q + shift // 128
            turn = shift % 128
            pieces = []
            for r in (row, row + 1):
                piece = match_ref[pl.ds(jnp.minimum(r, last), 1), :]
                piece = jnp.broadcast_to(piece, (8, 128))
                pieces.append(pltpu.roll(piece, (128 - turn) % 128, 1))
            found = jnp.where(lane < 128 - turn, pieces[0], pieces[1])
            here = q * 128 + lane
            tile = jnp.where((here >= y * ROWS) & (here < (y + 1) * ROWS), found, tile)
        tiles.append(tile)
    return jnp.concatenate(tiles, axis=1)[0:1, :SETS]


def weigh(lag, s_ref, labels, member, given, w_ref, lost_ref=None, first=True):
    factor, offset = given[0:1, 0:1] * LOG2E, given[0:1, 1:2] * LOG2E
    anchor = given[0:1, 2:3].astype(jnp.int32)
    turned = (anchor - lag) & (NBLK - 1)
    partner = member ^ (Y * CORE)
    bases = [turned * SPAN + member * ROWS, turned * SPAN + (partner - 1) * ROWS]

    def chunk(i, carry):
        start = pl.multiple_of(i * CHUNK, CHUNK)
        rows = start + lax.broadcasted_iota(jnp.int32, (CHUNK, 1), 0)
        base = jnp.where(rows < ROWS, bases[0], bases[1])
        logits = factor * s_ref[pl.ds(start, CHUNK), :] + offset
        paired = (rows + base) == labels
        t = jnp.where(paired, -logits, logits)
        e = jnp.exp2(-jnp.abs(t))
        more = jnp.where(e < 1e-4, LOG2E * e * (1.0 - 0.5 * e), jnp.log2(1.0 + e))
        lost = jnp.maximum(t, 0.0) + more
        sig = jnp.exp2(t - lost)
        w_ref[pl.ds(start, CHUNK), :] = jnp.where(paired, -sig, sig).astype(BF16)
        if lost_ref is not None:
            total = jnp.sum(lost, axis=1, keepdims=True)
            if not first:
                total = total + lost_ref[pl.ds(start, CHUNK), :]
            lost_ref[pl.ds(start, CHUNK), :] = total
        return carry

    lax.fori_loop(0, XH * ROWS // CHUNK, chunk, 0, unroll=True)


def logits_of(texts, images):
    return lax.dot_general(texts, images, (((1,), (1,)), ((), ())), preferred_element_type=F32)


def image_part(weights, texts):
    return lax.dot_general(weights, texts, (((0,), (0,)), ((), ())), preferred_element_type=F32)


def fetch(pairs, sems):
    copies = [pltpu.make_async_copy(a, b, sems.at[i]) for i, (a, b) in enumerate(pairs)]
    for copy in copies:
        copy.start()
    return copies


def own_logits(
    match, text, loss_hbm, given, t1, images, texts, s0, labels, loss_acc, match_v, sems
):
    copies = fetch([(match, match_v), (text, texts.at[:ROWS, :]), (loss_hbm, loss_acc)], sems)
    texts[ROWS:, :] = t1[...]
    for copy in copies:
        copy.wait()
    s0[...] = logits_of(texts[...], images[...])
    member = lax.axis_index("grp")
    at = lax.broadcasted_iota(jnp.int32, labels.shape, 0)
    labels[...] = jnp.where(at == 0, labels_of(match_v, member, 0), labels_of(match_v, member, 1))


def late_texts(texts0, z, d, texts):
    texts[:LAG, :] = texts0[...]
    texts[LAG : LAG + ROWS, :] = z[...]
    texts[LAG + ROWS :, :] = d[...]


def row_of(column):
    r = lax.broadcasted_iota(jnp.int32, (ROWS, 128), 0)
    c = lax.broadcasted_iota(jnp.int32, (ROWS, 128), 1)
    return jnp.sum(jnp.where(r == c, column, 0.0), axis=0, keepdims=True)


def loss_rows(lost):
    rows = [row_of(lost[i * ROWS : (i + 1) * ROWS, :]) * (LN2 / SPAN) for i in range(XH)]
    at = lax.broadcasted_iota(jnp.int32, (TAIL, 128), 0)
    return jnp.where(at == 0, rows[0], jnp.where(at == 1, rows[1], 0.0))


def first_lag(
    given, labels, texts, s_own, own, other, acc, loss_acc, w_own, sent, s, w_other, lost
):
    member = lax.axis_index("grp")
    s[...] = logits_of(texts[...], other[...])
    weigh(0, s_own, labels[0:1, :], member, given, w_own, lost, True)
    grad = jnp.dot(w_own[...], own[...], preferred_element_type=F32)
    weigh(0, s, labels[1:2, :], member, given, w_other, lost, False)
    grad = grad + jnp.dot(w_other[...], other[...], preferred_element_type=F32)
    grad = given[0:1, 0:1] * grad
    sent[:ROWS, :] = (acc[...] + grad[:ROWS]).astype(BF16)
    sent[ROWS : 2 * ROWS, :] = grad[ROWS:].astype(BF16)
    at = lax.broadcasted_iota(jnp.int32, (TAIL, ROWS), 0)
    tail = loss_rows(lost)[:, :ROWS] + jnp.where(at == 0, loss_acc[...], 0.0)
    sent[2 * ROWS :, :] = jnp.zeros((TAIL, sent.shape[1]), BF16)
    sent[2 * ROWS :, :ROWS] = tail.astype(BF16)


def second_lag(
    given, labels, texts, own, other, w_own, late, late_rows, s_own, s, w_other, lost
):
    member = lax.axis_index("grp")
    s_own[...] = logits_of(texts[LAG:, :], own[...])
    s[...] = logits_of(texts[LAG:, :], other[...])
    weigh(1, s_own, labels[0:1, :], member, given, w_own, lost, True)
    grad = jnp.dot(w_own[...], own[...], preferred_element_type=F32)
    weigh(1, s, labels[1:2, :], member, given, w_other, lost, False)
    grad = grad + jnp.dot(w_other[...], other[...], preferred_element_type=F32)
    late[...] = given[0:1, 0:1] * grad
    late_rows[...] = loss_rows(lost)[:8, :]


def image_parts(
    given, labels, w0, w1, texts, beside, own, token, kept, one, two, three, s_b, w, w_b, total
):
    member = lax.axis_index("grp")
    there = member ^ 1
    row = labels[0:1, :]
    s_b[...] = logits_of(beside[...], own[...])
    w[:LAG, :] = w0[...]
    w[LAG:, :] = w1[...]
    total[...] = image_part(w[...], texts[...])
    weigh(0, s_b.at[:LAG, :], row, there, given, w_b.at[:LAG, :])
    weigh(1, s_b.at[LAG:, :], row, there, given, w_b.at[LAG:, :])
    total[...] += image_part(w_b[...], beside[...])
    factor = given[0:1, 0:1]
    y = (member // CORE) & (Y - 1)
    for step, out in zip(STEPS, (kept, one, two, three)):
        start = pl.multiple_of(((y + step) & (Y - 1)) * ROWS, 16)
        out[...] = (factor * total[pl.ds(start, ROWS), :]).astype(out.dtype)


def across(late, late_rows, came, sent):
    sent[:ROWS, :] = (late[ROWS:, :] + came[ROWS : 2 * ROWS, :].astype(F32)).astype(BF16)
    sent[ROWS:, :] = jnp.zeros((TAIL, sent.shape[1]), BF16)
    tail = came[2 * ROWS :, :128].astype(F32)
    sent[ROWS:, :128] = (tail[1:2, :] + late_rows[1:2, :] + jnp.zeros((TAIL, 128), F32)).astype(BF16)


def image_end(kept, one, two, three, out, token):
    token[...] = kept[:8, :128]
    out[...] = kept[...] + one[...].astype(F32) + two[...].astype(F32) + three[...].astype(F32)


def text_end(late, late_rows, came, crossed, token, grad, loss):
    grad[...] = late[:ROWS, :] + came[:ROWS, :].astype(F32) + crossed[:ROWS, :].astype(F32)
    ahead = came[2 * ROWS :, :128].astype(F32)
    beside = crossed[ROWS:, :128].astype(F32)
    loss[...] = (late_rows[0:1, :] + ahead[0:1, :] + beside[0:1, :])[:, :ROWS]


def on_device(image_emb, text_held, text_grad_acc, text_loss_acc, match, step, scale, bias):
    width = text_held.shape[1]

    text_z = to_next_group(text_held, stay)
    text_d = to_next_group(text_held, across_x)
    text_x = to_member(text_held, across_x)
    images = gather_y(image_emb)
    images_other = to_member(images, across_core)

    match = match.reshape(-1, 128)
    anchor = (lax.axis_index("blk").astype(jnp.int32) - step) & (NBLK - 1)
    given = jnp.concatenate([scale, bias, anchor.astype(F32), jnp.zeros((125,), F32)]).reshape(1, 128)

    big = 2 * LAG * SETS * width
    block = shape(ROWS, width, BF16)
    logits = held(LAG, SETS, F32)
    weights = held(LAG, SETS, BF16)
    texts0, s0, labels, loss_acc = call(
        own_logits,
        [shape(LAG, width, BF16), logits, held(8, SETS, jnp.int32), held(1, ROWS, F32)],
        [match, text_held, text_loss_acc.reshape(1, ROWS), given, text_x, images],
        2 * big,
        [pltpu.VMEM(match.shape, jnp.int32), pltpu.SemaphoreType.DMA((3,))],
        far=3,
    )
    w0, ahead = call(
        first_lag,
        [weights, shape(LAG + TAIL, width, BF16)],
        [given, labels, texts0, s0, images, images_other, text_grad_acc, loss_acc],
        3 * big,
        [logits, weights, held(LAG, 1, F32)],
    )
    came = to_next_group(ahead, stay)
    (texts,) = call(late_texts, [shape(2 * LAG, width, BF16)], [texts0, text_z, text_d], big // 8)
    texts_beside = to_member(texts, across_core)
    w1, late, late_rows = call(
        second_lag,
        [weights, held(LAG, width, F32), held(8, 128, F32)],
        [given, labels, texts, images, images_other],
        4 * big,
        [logits, logits, weights, held(LAG, 1, F32)],
    )
    kept, *sent = call(
        image_parts,
        [held(ROWS, width, F32), block, block, block],
        [given, labels, w0, w1, texts, texts_beside, images, late_rows],
        6 * big,
        [held(2 * LAG, SETS, F32), held(2 * LAG, SETS, BF16), held(2 * LAG, SETS, BF16), held(SETS, width, F32)],
    )
    arrived = [to_member(part, along_y(i)) for i, part in zip(STEPS[1:], sent)]
    (crossing,) = call(across, [shape(ROWS + TAIL, width, BF16)], [late, late_rows, came], ROWS * width)
    crossed = to_member(crossing, across_x)
    image_grad, token = call(
        image_end, [shape(ROWS, width, F32), held(8, 128, F32)], [kept, *arrived], 40 * big
    )
    text_grad_out, loss = call(
        text_end,
        [shape(ROWS, width, F32), shape(1, ROWS, F32)],
        [late, late_rows, came, crossed, token],
        ROWS * width,
    )
    return (image_grad, text_grad_out, loss.reshape(ROWS))


def solution(mesh):
    placed = (
        P(("blk", "grp"), None),
        P(("blk", "grp"), None),
        P(("blk", "grp"), None),
        P(("blk", "grp")),
        P("blk"),
        P(),
        P(),
        P(),
    )
    return jax.shard_map(
        on_device,
        mesh=mesh,
        in_specs=placed,
        out_specs=(P(("blk", "grp"), None), P(("blk", "grp"), None), P(("blk", "grp"))),
        check_vma=False,
    )
```
